128 devices in a mesh: section: 16 (over x_hi, z, core), tp: 8 (over x_lo, y).
Axes of the slice: x: 4 (x_hi: 2, x_lo: 2; x = x_hi * 2 + x_lo), y: 4, z: 4, core: 2. Of those that a mesh axis runs over, the one named last changes fastest.
Arguments:
- arrivals: bfloat16 [16, 256, 4096], P('section', None, 'tp'), may hold values from -6 to 6
- fresh_inputs: bfloat16 [1, 256, 4096], P(None, None, 'tp'), may hold values from -6 to 6
- returning: bfloat16 [16, 256, 4096], P('section', None, 'tp'), may hold values from -0.625 to 0.625
- loss_grads: bfloat16 [1, 256, 4096], P(None, None, 'tp'), may hold values from -0.625 to 0.625
- stash_rows: bfloat16 [16, 2, 256, 4096], P('section', None, None, 'tp'), may hold values from -0.625 to 0.625
- forward_docs: int32 [17, 256], replicated, may hold values from 0 to 3, never falling along the last dimension, each value on 1 to 128 neighbouring positions
- backward_docs: int32 [17, 256], replicated, may hold values from 0 to 3, never falling along the last dimension, each value on 1 to 128 neighbouring positions
- norm_gain: float32 [16, 4096], P('section'), may hold values from 0.5 to 1.5
- w_query: bfloat16 [16, 4096, 4096], P('section', None, 'tp'), may hold values from -0.09375 to 0.09375
- w_key: bfloat16 [16, 4096, 1024], P('section', None, 'tp'), may hold values from -0.09375 to 0.09375
- w_value: bfloat16 [16, 4096, 1024], P('section', None, 'tp'), may hold values from -0.09375 to 0.09375
- w_out: bfloat16 [16, 4096, 4096], P('section', 'tp'), may hold values from -0.09375 to 0.09375
Outputs:
- forward_out: bfloat16 [16, 2, 256, 4096], P('section', None, None, 'tp')
- backward_out: float32 [16, 2, 256, 4096], P('section', None, None, 'tp')
- evicted: bfloat16 [16, 2, 256, 4096], P('section', None, None, 'tp')
- grad_query: bfloat16 [16, 4096, 4096], P('section', None, 'tp')
- grad_key: bfloat16 [16, 4096, 1024], P('section', None, 'tp')
- grad_value: bfloat16 [16, 4096, 1024], P('section', None, 'tp')
- grad_out: bfloat16 [16, 4096, 4096], P('section', 'tp')
- grad_gain: float32 [16, 4096], P('section', 'tp')
The draws below stay inside these ranges and needn't reach their ends.
Inputs may be any that keep to these rules, and one draw needn't show every extreme that they name: `forward_docs`: in each row document numbers never fall, run over 0 to 3, and each document is 1 to 128 tokens long. `backward_docs`: in each row document numbers never fall, run over 0 to 3, and each document is 1 to 128 tokens long.
All inputs are finite; a program needn't handle non-finite values.
Results may differ from the reference program's by a relative error of at most 0.02.
Values may be sent and summed in bfloat16 or wider, within the bound.
No kernel may reach another device: no remote copies, remote signals or barrier semaphores. Data moves between devices by JAX's collectives and lax.ppermute only.
A program may use at most 192 MiB of HBM per device.

```python
import math
import jax
import jax.numpy as jnp
import numpy as np
from jax import lax

D = 4096
HEADS = 32
KVH = 8
DH = 128
SEQ = 256
TICKS = 2
DOCS = 4
SECTIONS = 16
BLOCKS = 17
DOC_MOST = 128


def level_of(stream_key, dims, split, least, top_value):
    def one(dim, blocks):
        heights = jax.random.uniform(jax.random.fold_in(jax.random.fold_in(stream_key, 6), dim), (blocks,), jnp.float32, least / len(split), top_value / len(split))
        return jnp.repeat(jnp.exp(heights), dims[dim] // blocks).reshape((-1,) + (1,) * (len(dims) - dim - 1))

    factor_of = one(*split[0])
    for cut in split[1:]:
        factor_of = factor_of * one(*cut)
    return factor_of


def split_up(amount, total, most, slope):
    loads = [(1 << 20) // math.isqrt(grade ** slope) + 1 for grade in range(2, amount + 1)]
    surplus, holding = total - most - (amount - 1), [1] * (amount - 1)
    while surplus > 0:
        candidates = [i for i in range(amount - 1) if holding[i] < most]
        mass, left = sum([loads[i] for i in candidates]), surplus
        for i in candidates:
            more = min(most - holding[i], max(1, left * loads[i] // mass), surplus)
            holding[i] = holding[i] + more
            surplus = surplus - more
    return np.array([most] + holding)


def ragged(own_key, amount, total, reach, lean):
    if amount == 2:
        one = jax.random.randint(own_key, (), max(1, total - reach), min(reach, total - 1) + 1)
        return jnp.stack([one, total - one])
    sizes = jnp.asarray(split_up(amount, total, reach, lean), jnp.int32)
    pairs = (amount - 1) // 2
    donor, receiver = sizes[1:1 + 2 * pairs:2], sizes[2:2 + 2 * pairs:2]
    margin = jnp.minimum(donor - 1, reach - receiver)
    moved = jax.random.randint(jax.random.fold_in(own_key, 1), (pairs,), 0, 1 << 20) % (margin + 1)
    sizes = sizes.at[1:1 + 2 * pairs:2].set(donor - moved).at[2:2 + 2 * pairs:2].set(receiver + moved)
    return sizes[jax.random.permutation(jax.random.fold_in(own_key, 2), amount)]


def centred(stream_key, extent, scale, most, split=(), held_as=jnp.bfloat16):
    values = scale * jax.random.normal(stream_key, extent, jnp.float32)
    if split:
        values = values * level_of(stream_key, extent, split, -0.22, 0.18)
    return jnp.clip(values, -most, most).astype(held_as)


def setup_inputs(seed: int = 0) -> dict:
    key_list = jax.random.split(jax.random.key(seed), 13)
    return {
        "arrivals": centred(key_list[0], (SECTIONS, SEQ, D), 1.0, 6.0, ((0, 16), (2, 8))),
        "fresh_inputs": centred(key_list[1], (TICKS - 1, SEQ, D), 1.0, 6.0, ((2, 8),)),
        "returning": centred(key_list[2], (SECTIONS, SEQ, D), 0.1, 0.625, ((0, 16), (2, 8))),
        "loss_grads": centred(key_list[3], (TICKS - 1, SEQ, D), 0.1, 0.625, ((2, 8),)),
        "stash_rows": centred(key_list[4], (SECTIONS, TICKS, SEQ, D), 0.1, 0.625, ((0, 16), (3, 8))),
        "forward_docs": jax.vmap(lambda own: jnp.searchsorted(jnp.cumsum(ragged(own, DOCS, SEQ, DOC_MOST, 1)), jnp.arange(SEQ), side="right"))(jax.random.split(key_list[5], BLOCKS)).reshape((BLOCKS, SEQ)).astype(jnp.int32),
        "backward_docs": jax.vmap(lambda own: jnp.searchsorted(jnp.cumsum(ragged(own, DOCS, SEQ, DOC_MOST, 1)), jnp.arange(SEQ), side="right"))(jax.random.split(key_list[6], BLOCKS)).reshape((BLOCKS, SEQ)).astype(jnp.int32),
        "norm_gain": jnp.clip(1.0 + 0.1 * jax.random.normal(key_list[7], (SECTIONS, D), jnp.float32), 0.5, 1.5),
        "w_query": centred(key_list[8], (SECTIONS, D, HEADS * DH), D ** -0.5, 0.09375, ((0, 16), (2, 8))),
        "w_key": centred(key_list[9], (SECTIONS, D, KVH * DH), D ** -0.5, 0.09375, ((0, 16), (2, 8))),
        "w_value": centred(key_list[10], (SECTIONS, D, KVH * DH), D ** -0.5, 0.09375, ((0, 16), (2, 8))),
        "w_out": centred(key_list[11], (SECTIONS, HEADS * DH, D), (HEADS * DH) ** -0.5, 0.09375, ((0, 16), (1, 8))),
    }


EPSILON = 1e-05
NEGATIVE = -1e+30

def doc_mask(segment_ids):
    places = jnp.arange(segment_ids.shape[0])
    same = segment_ids[:, None] == segment_ids[None, :]
    return same & (places[None, :] <= places[:, None])

def normalize(rows_in, norm_row):
    values = rows_in.astype(jnp.float32)
    inverse = lax.rsqrt(lax.optimization_barrier(jnp.mean(values * values, axis=-1, keepdims=True)) + EPSILON)
    unit_rows = values * inverse
    return (unit_rows, inverse, (unit_rows * norm_row).astype(jnp.bfloat16))

def attend(normed, query_weight, key_weight, value_weight, allowed):
    length = normed.shape[0]
    query = jnp.dot(normed, query_weight, preferred_element_type=jnp.float32).astype(jnp.bfloat16)
    keys = jnp.dot(normed, key_weight, preferred_element_type=jnp.float32).astype(jnp.bfloat16)
    values = jnp.dot(normed, value_weight, preferred_element_type=jnp.float32).astype(jnp.bfloat16)
    kv_heads = keys.shape[1] // DH
    groups = query.shape[1] // keys.shape[1]
    query_heads = query.astype(jnp.float32).reshape(length, kv_heads, groups, DH)
    key_heads = keys.astype(jnp.float32).reshape(length, kv_heads, DH)
    value_heads = values.astype(jnp.float32).reshape(length, kv_heads, DH)
    scores = jnp.einsum('skgd,tkd->kgst', query_heads, key_heads) * DH ** (-0.5)
    scores = jnp.where(allowed, scores, NEGATIVE)
    probability = jax.nn.softmax(scores, axis=-1)
    weights = probability.astype(jnp.bfloat16)
    mixed_rows = jnp.einsum('kgst,tkd->skgd', weights.astype(jnp.float32), value_heads)
    mixed_rows = mixed_rows.reshape(length, -1).astype(jnp.bfloat16)
    return (query_heads, key_heads, value_heads, probability, weights, mixed_rows)

def section_forward(rows_in, norm_row, query_weight, key_weight, value_weight, out_weight, allowed):
    normed = normalize(rows_in, norm_row)[2]
    mixed_rows = attend(normed, query_weight, key_weight, value_weight, allowed)[5]
    attention = jnp.dot(mixed_rows, out_weight, preferred_element_type=jnp.float32)
    return (rows_in.astype(jnp.float32) + attention).astype(jnp.bfloat16)

def section_backward(rows_in, cotangent, norm_row, query_weight, key_weight, value_weight, out_weight, allowed):
    unit_rows, inverse, normed = normalize(rows_in, norm_row)
    query_heads, key_heads, value_heads, probability, weights, mixed_rows = attend(normed, query_weight, key_weight, value_weight, allowed)
    length = normed.shape[0]
    g_rounded = cotangent.astype(jnp.bfloat16)
    d_mixed = jnp.dot(g_rounded, out_weight.T, preferred_element_type=jnp.float32).astype(jnp.bfloat16)
    grad_out = jnp.dot(mixed_rows.T, g_rounded, preferred_element_type=jnp.float32)
    d_heads = d_mixed.astype(jnp.float32).reshape(query_heads.shape)
    d_probability = jnp.einsum('skgd,tkd->kgst', d_heads, value_heads)
    inner = lax.optimization_barrier(jnp.sum(d_probability * probability, axis=-1, keepdims=True))
    d_scores = (probability * (d_probability - inner) * DH ** (-0.5)).astype(jnp.bfloat16)
    score_grads = d_scores.astype(jnp.float32)
    d_query = jnp.einsum('kgst,tkd->skgd', score_grads, key_heads).reshape(length, -1).astype(jnp.bfloat16)
    d_keys = jnp.einsum('kgst,skgd->tkd', score_grads, query_heads).reshape(length, -1).astype(jnp.bfloat16)
    d_values = jnp.einsum('kgst,skgd->tkd', weights.astype(jnp.float32), d_heads).reshape(length, -1).astype(jnp.bfloat16)
    grad_query = jnp.dot(normed.T, d_query, preferred_element_type=jnp.float32)
    grad_key = jnp.dot(normed.T, d_keys, preferred_element_type=jnp.float32)
    grad_value = jnp.dot(normed.T, d_values, preferred_element_type=jnp.float32)
    d_normed = jnp.dot(d_query, query_weight.T, preferred_element_type=jnp.float32)
    d_normed = d_normed + jnp.dot(d_keys, key_weight.T, preferred_element_type=jnp.float32)
    d_normed = d_normed + jnp.dot(d_values, value_weight.T, preferred_element_type=jnp.float32)
    d_unit = d_normed * norm_row
    d_rows = inverse * (d_unit - unit_rows * lax.optimization_barrier(jnp.mean(d_unit * unit_rows, axis=-1, keepdims=True)))
    passed = cotangent + d_rows
    grad_norm = lax.optimization_barrier(jnp.sum(d_normed * unit_rows, axis=0))
    return (passed, grad_query, grad_key, grad_value, grad_out, grad_norm)

def reference(arrivals, fresh_inputs, returning, loss_grads, stash_rows, forward_docs, backward_docs, norm_gain, w_query, w_key, w_value, w_out):
    inputs_at = []
    outputs_at = []
    for layer_index in range(SECTIONS):
        series_in = []
        series_out = []
        for moment in range(TICKS):
            if moment == 0:
                incoming = arrivals[layer_index]
            elif layer_index == 0:
                incoming = fresh_inputs[moment - 1]
            else:
                incoming = outputs_at[layer_index - 1][moment - 1]
            allowed = doc_mask(forward_docs[moment - layer_index + SECTIONS - 1])
            series_in.append(incoming)
            series_out.append(section_forward(incoming, norm_gain[layer_index], w_query[layer_index], w_key[layer_index], w_value[layer_index], w_out[layer_index], allowed))
        inputs_at.append(series_in)
        outputs_at.append(series_out)
    passed_at = [None] * SECTIONS
    grads_at = [None] * SECTIONS
    for layer_index in range(SECTIONS - 1, -1, -1):
        series_back = []
        totals = None
        for moment in range(TICKS):
            if moment == 0:
                cotangent = returning[layer_index].astype(jnp.float32)
            elif layer_index == SECTIONS - 1:
                cotangent = loss_grads[moment - 1].astype(jnp.float32)
            else:
                cotangent = passed_at[layer_index + 1][moment - 1]
            allowed = doc_mask(backward_docs[moment + layer_index])
            results = section_backward(stash_rows[SECTIONS - 1 - layer_index, moment], cotangent, norm_gain[layer_index], w_query[layer_index], w_key[layer_index], w_value[layer_index], w_out[layer_index], allowed)
            series_back.append(results[0])
            if totals is None:
                totals = results[1:]
            else:
                totals = jax.tree.map(jnp.add, totals, results[1:])
        passed_at[layer_index] = series_back
        grads_at[layer_index] = tuple((item.astype(jnp.bfloat16) for item in totals[:4])) + (totals[4],)
    forward_out = jnp.stack([jnp.stack(series) for series in outputs_at])
    backward_out = jnp.stack([jnp.stack(series) for series in passed_at])
    evicted = jnp.stack([jnp.stack(inputs_at[SECTIONS - 1 - index]) for index in range(SECTIONS)])
    grad_query = jnp.stack([entry[0] for entry in grads_at])
    grad_key = jnp.stack([entry[1] for entry in grads_at])
    grad_value = jnp.stack([entry[2] for entry in grads_at])
    grad_out = jnp.stack([entry[3] for entry in grads_at])
    grad_gain = jnp.stack([entry[4] for entry in grads_at])
    return (forward_out, backward_out, evicted, grad_query, grad_key, grad_value, grad_out, grad_gain)
```

```python
import functools

import jax
import jax.numpy as jnp
from jax import lax
from jax.experimental import pallas as pl
from jax.experimental.pallas import tpu as pltpu
from jax.sharding import PartitionSpec as P

DH = 128
ROWS = 4
EPSILON = 1e-05
NEGATIVE = -1e30
F32 = jnp.float32
BF16 = jnp.bfloat16
VMEM = pl.BlockSpec(memory_space=pltpu.VMEM)
ANY = pl.BlockSpec(memory_space=pl.ANY)
PARAMS = pltpu.CompilerParams(vmem_limit_bytes=48 * 1024 * 1024)


def shifted(block, distance):
    devices = range(lax.axis_size("section"))
    route = [(i - distance, i) for i in devices if i - distance in devices]
    return lax.ppermute(block, "section", route)


def mirrored(block):
    count = lax.axis_size("section")
    return lax.ppermute(block, "section", [(i, count - 1 - i) for i in range(count)])


def x_flip(value):
    return lax.ppermute(value, "tp", [(i, i ^ ROWS) for i in range(2 * ROWS)])


def y_from(value, step):
    route = [(i, (i & ROWS) | ((i - step) % ROWS)) for i in range(2 * ROWS)]
    return lax.ppermute(value, "tp", route)


def gather_x_first(own):
    other = x_flip(own)
    pair = jnp.stack([own, other])
    entries = [(own, None, 0, 0), (other, None, 1, 0)]
    for dy in (1, 3, 2):
        got = y_from(pair, dy)
        entries += [(got, 0, 0, dy), (got, 1, 1, dy)]
    return entries


def gather_y_first(own):
    other = x_flip(own)
    rows = [y_from(own, dy) for dy in (1, 3, 2)]
    trio = x_flip(jnp.stack(rows))
    entries = [(own, None, 0, 0), (other, None, 1, 0)]
    for i, dy in enumerate((1, 3, 2)):
        entries += [(rows[i], None, 0, dy), (trio, i, 1, dy)]
    return entries


X_LAST = tuple(((0, dy), (1, dy)) for dy in range(ROWS))
X_FIRST = tuple(tuple((dx, dy) for dy in range(ROWS)) for dx in range(2))


def scatter_x_last(parts):
    got = [parts[0]] + [y_from(parts[dy], -dy) for dy in (1, 3, 2)]
    leaving = sum(g[1].astype(F32) for g in got).astype(BF16)
    other = x_flip(leaving)
    return sum(g[0].astype(F32) for g in got) + other.astype(F32)


def scatter_x_first(parts):
    arrived = x_flip(parts[1])
    merged = [
        (parts[0][dy].astype(F32) + arrived[dy].astype(F32)) for dy in range(ROWS)
    ]
    got = [y_from(merged[dy].astype(BF16), -dy) for dy in (1, 3, 2)]
    return merged[0] + sum(g.astype(F32) for g in got)


def place(dx, dy, share):
    me = lax.axis_index("tp")
    x = lax.div(me, ROWS)
    y = lax.rem(me, ROWS)
    far_x = 1 - x if dx else x
    index = far_x * ROWS + lax.rem(y + dy, ROWS)
    return pl.multiple_of(index * share, share)


def operands_of(entries):
    arrays, where = [], []
    for array, lead, dx, dy in entries:
        for i, known in enumerate(arrays):
            if known is array:
                break
        else:
            i = len(arrays)
            arrays.append(array)
        where.append((i, lead, dx, dy))
    return arrays, tuple(where)


def piece(refs, entry):
    ref, lead = refs[entry[0]], entry[1]
    return ref[...] if lead is None else ref[lead]


def dot(a, b, dims=((1,), (0,))):
    return lax.dot_general(a, b, (dims, ((), ())), preferred_element_type=F32)


NT = ((1,), (1,))
TN = ((0,), (0,))


def mask_of(docs_ref, row):
    ids = docs_ref[pl.ds(row, 1), :]
    length = ids.shape[1]
    p = lax.broadcasted_iota(jnp.int32, (length, length), 0)
    r = lax.broadcasted_iota(jnp.int32, (length, length), 1)
    across = jnp.broadcast_to(ids, (length, length))
    down = jnp.sum(jnp.where(p == r, across, 0), axis=1, keepdims=True)
    return (across == down) & (r <= p)


def normalize_into(x_refs, where, gain_ref, normed_ref):
    width = gain_ref.shape[1]
    share = width // len(where)
    total = None
    for entry in where:
        v = piece(x_refs, entry).astype(F32)
        s = jnp.sum(v * v, axis=-1, keepdims=True)
        total = s if total is None else total + s
    inverse = lax.rsqrt(total / width + EPSILON)
    for entry in where:
        at = place(entry[2], entry[3], share)
        v = piece(x_refs, entry).astype(F32) * inverse
        normed_ref[:, pl.ds(at, share)] = (v * gain_ref[:, pl.ds(at, share)]).astype(BF16)
    return inverse


def attention(qkv, allowed, heads):
    k = qkv[:, heads * DH : (heads + 1) * DH]
    v = qkv[:, (heads + 1) * DH :]
    probs, mixed = [], []
    for h in range(heads):
        s = dot(qkv[:, h * DH : (h + 1) * DH], k, NT) * DH ** (-0.5)
        s = jnp.where(allowed, s, NEGATIVE)
        e = jnp.exp(s - jnp.max(s, axis=-1, keepdims=True))
        p = e / jnp.sum(e, axis=-1, keepdims=True)
        probs.append(p)
        mixed.append(dot(p.astype(BF16), v).astype(BF16))
    return probs, jnp.concatenate(mixed, axis=1)


def project(normed_ref, wq_ref, wk_ref, wv_ref):
    normed = normed_ref[...]
    q = dot(normed, wq_ref[...])
    kv = dot(normed, jnp.concatenate([wk_ref[...], wv_ref[...]], axis=1))
    return jnp.concatenate([q, kv], axis=1).astype(BF16)


def loads(sources, scratch, sems):
    copies = [
        pltpu.make_async_copy(source, target, sems.at[i])
        for i, (source, target) in enumerate(zip(sources, scratch))
    ]
    for copy in copies:
        copy.start()
    return copies


def forward_kernel(tick, where, layout, n_x, *refs):
    x_refs, refs = refs[:n_x], refs[n_x:]
    docs, gain, wq_hbm, wk_hbm, wv_hbm, wo_hbm = refs[:6]
    outs, refs = refs[6 : 6 + len(layout)], refs[6 + len(layout) :]
    normed, wq, wk, wv, wo, sems = refs
    copies = loads((wq_hbm, wk_hbm, wv_hbm, wo_hbm), (wq, wk, wv, wo), sems)
    normalize_into(x_refs, where, gain, normed)
    row = tick + lax.axis_size("section") - 1 - lax.axis_index("section")
    allowed = mask_of(docs, row)
    for copy in copies[:3]:
        copy.wait()
    qkv = project(normed, wq, wk, wv)
    mixed = attention(qkv, allowed, wq.shape[1] // DH)[1]
    copies[3].wait()
    share = gain.shape[1] // len(where)
    for out, targets in zip(outs, layout):
        for lead, (dx, dy) in enumerate(targets):
            at = place(dx, dy, share)
            out[lead] = dot(mixed, wo[:, pl.ds(at, share)]).astype(BF16)


def recall_kernel(tick, where, n_x, *refs):
    x_refs, refs = refs[:n_x], refs[n_x:]
    docs, gain, wq_hbm, wk_hbm, wv_hbm = refs[:5]
    normed, inverse, qkv_out, probs_out, mixed_out = refs[5:10]
    wq, wk, wv, sems = refs[10:]
    copies = loads((wq_hbm, wk_hbm, wv_hbm), (wq, wk, wv), sems)
    inverse[...] = normalize_into(x_refs, where, gain, normed)
    allowed = mask_of(docs, tick + lax.axis_index("section"))
    for copy in copies:
        copy.wait()
    qkv = project(normed, wq, wk, wv)
    probs, mixed = attention(qkv, allowed, wq.shape[1] // DH)
    qkv_out[...] = qkv
    mixed_out[...] = mixed
    for h, p in enumerate(probs):
        probs_out[h] = p


def backward_kernel(where_g, n_g, where_x, n_x, layout, *refs):
    g_refs, refs = refs[:n_g], refs[n_g:]
    x_refs, refs = refs[:n_x], refs[n_x:]
    inverse_ref, qkv_ref, probs_ref, gain, wq_hbm, wk_hbm, wv_hbm, wo_hbm = refs[:8]
    outs, refs = refs[8 : 8 + len(layout)], refs[8 + len(layout) :]
    d_qkv_out, g_all, gain_out = refs[:3]
    wq, wk, wv, wo, sems = refs[3:]
    copies = loads((wo_hbm, wq_hbm, wk_hbm, wv_hbm), (wo, wq, wk, wv), sems)
    width = gain.shape[1]
    share = width // len(where_g)
    for entry in where_g:
        at = place(entry[2], entry[3], share)
        g_all[:, pl.ds(at, share)] = piece(g_refs, entry)
    copies[0].wait()
    d_mixed = dot(g_all[...], wo[...], NT).astype(BF16)
    heads = wq.shape[1] // DH
    k = qkv_ref[:, heads * DH : (heads + 1) * DH]
    v = qkv_ref[:, (heads + 1) * DH :]
    d_parts = []
    d_k = d_v = None
    for h in range(heads):
        q = qkv_ref[:, h * DH : (h + 1) * DH]
        p = probs_ref[h]
        d_out = d_mixed[:, h * DH : (h + 1) * DH]
        d_p = dot(d_out, v, NT)
        inner = jnp.sum(d_p * p, axis=-1, keepdims=True)
        d_s = (p * (d_p - inner) * DH ** (-0.5)).astype(BF16)
        d_parts.append(dot(d_s, k).astype(BF16))
        more_k = dot(d_s, q, TN)
        more_v = dot(p.astype(BF16), d_out, TN)
        d_k = more_k if d_k is None else d_k + more_k
        d_v = more_v if d_v is None else d_v + more_v
    d_qkv = jnp.concatenate(d_parts + [d_k.astype(BF16), d_v.astype(BF16)], axis=1)
    d_qkv_out[...] = d_qkv
    row_total = jnp.sum(d_qkv.astype(F32) * qkv_ref[...].astype(F32), axis=-1, keepdims=True)
    row_mean = row_total / width
    inverse = inverse_ref[...]
    for copy in copies[1:]:
        copy.wait()
    found = {(entry[2], entry[3]): entry for entry in where_x}
    d_q, d_kv = d_qkv[:, : heads * DH], d_qkv[:, heads * DH :]
    for out, targets in zip(outs, layout):
        for lead, (dx, dy) in enumerate(targets):
            at = place(dx, dy, share)
            rows = pl.ds(at, share)
            w_kv = jnp.concatenate([wk[rows, :], wv[rows, :]], axis=1)
            d_normed = dot(d_q, wq[rows, :], NT) + dot(d_kv, w_kv, NT)
            unit = piece(x_refs, found[dx, dy]).astype(F32) * inverse
            gain_out[dx * ROWS + dy] = jnp.sum(d_normed * unit, axis=0, keepdims=True)
            d_unit = d_normed * gain[:, rows]
            out[lead] = (inverse * (d_unit - unit * row_mean)).astype(BF16)


def grads_kernel(n0, n1, dq0, dq1, m0, m1, g0, g1, gq, gk, gv, go):
    d0, d1 = dq0[...], dq1[...]
    grad = dot(n0[...], d0, TN) + dot(n1[...], d1, TN)
    wide = gq.shape[1]
    gq[...] = grad[:, :wide].astype(BF16)
    gk[...] = grad[:, wide : wide + DH].astype(BF16)
    gv[...] = grad[:, wide + DH :].astype(BF16)
    go[...] = (dot(m0[...], g0[...], TN) + dot(m1[...], g1[...], TN)).astype(BF16)


def shape(dims, dtype=BF16):
    return jax.ShapeDtypeStruct(dims, dtype)


def cost(multiplies, moved):
    return pl.CostEstimate(flops=2 * multiplies, bytes_accessed=moved, transcendentals=0)


def part_shapes(layout, length, share):
    return [shape((len(targets), length, share)) for targets in layout]


def scratch_for(*weights):
    return [pltpu.VMEM(w.shape, w.dtype) for w in weights] + [
        pltpu.SemaphoreType.DMA((len(weights),))
    ]


def forward_parts(tick, entries, layout, docs, gain, wq, wk, wv, wo):
    arrays, where = operands_of(entries)
    length, share = entries[0][0].shape
    width = gain.shape[1]
    own = wq.shape[1] + wk.shape[1] + wv.shape[1]
    return pl.pallas_call(
        functools.partial(forward_kernel, tick, where, layout, len(arrays)),
        out_shape=part_shapes(layout, length, share),
        in_specs=[VMEM] * (len(arrays) + 2) + [ANY] * 4,
        out_specs=[VMEM] * len(layout),
        scratch_shapes=[pltpu.VMEM((length, width), BF16)] + scratch_for(wq, wk, wv, wo),
        compiler_params=PARAMS,
        cost_estimate=cost(length * width * (own + wo.shape[0]), 2 * width * (own + wo.shape[0])),
        name="forward",
    )(*arrays, docs, gain, wq, wk, wv, wo)


def recall(tick, entries, docs, gain, wq, wk, wv):
    arrays, where = operands_of(entries)
    length = entries[0][0].shape[0]
    width = gain.shape[1]
    own = wq.shape[1] + wk.shape[1] + wv.shape[1]
    return pl.pallas_call(
        functools.partial(recall_kernel, tick, where, len(arrays)),
        out_shape=[
            shape((length, width)),
            shape((length, 1), F32),
            shape((length, own)),
            shape((wq.shape[1] // DH, length, length), F32),
            shape((length, wq.shape[1])),
        ],
        in_specs=[VMEM] * (len(arrays) + 2) + [ANY] * 3,
        out_specs=[VMEM] * 5,
        scratch_shapes=scratch_for(wq, wk, wv),
        compiler_params=PARAMS,
        cost_estimate=cost(length * width * own, 2 * width * own),
        name="recall",
    )(*arrays, docs, gain, wq, wk, wv)


def backward_parts(entries_g, entries_x, layout, inverse, qkv, probs, gain, wq, wk, wv, wo):
    arrays_g, where_g = operands_of(entries_g)
    arrays_x, where_x = operands_of(entries_x)
    length, share = entries_g[0][0].shape
    width = gain.shape[1]
    own = qkv.shape[1]
    results = pl.pallas_call(
        functools.partial(
            backward_kernel, where_g, len(arrays_g), where_x, len(arrays_x), layout
        ),
        out_shape=part_shapes(layout, length, share)
        + [
            shape((length, own)),
            shape((length, width)),
            shape((width // share, 1, share), F32),
        ],
        in_specs=[VMEM] * (len(arrays_g) + len(arrays_x) + 4) + [ANY] * 4,
        out_specs=[VMEM] * (len(layout) + 3),
        scratch_shapes=scratch_for(wq, wk, wv, wo),
        compiler_params=PARAMS,
        cost_estimate=cost(length * width * (own + wo.shape[0]), 2 * width * (own + wo.shape[0])),
        name="backward",
    )(*arrays_g, *arrays_x, inverse, qkv, probs, gain, wq, wk, wv, wo)
    parts = results[: len(layout)]
    return (parts, *results[len(layout) :])


def weight_grads(normed, d_qkv, mixed, g_all, wq, wk, wv, wo):
    length, width = normed[0].shape
    block = min(512, width)
    whole = lambda a: pl.BlockSpec(a.shape, lambda i: (0, 0))
    slab = pl.BlockSpec((length, block), lambda i: (0, i))
    rows = lambda w: pl.BlockSpec((block, w.shape[1]), lambda i: (i, 0))
    own = d_qkv[0].shape[1]
    return pl.pallas_call(
        grads_kernel,
        grid=(width // block,),
        out_shape=[shape(w.shape) for w in (wq, wk, wv, wo)],
        in_specs=[slab, slab, whole(d_qkv[0]), whole(d_qkv[0]), whole(mixed[0]), whole(mixed[0]), slab, slab],
        out_specs=[rows(wq), rows(wk), rows(wv), pl.BlockSpec((wo.shape[0], block), lambda i: (0, i))],
        compiler_params=PARAMS,
        cost_estimate=cost(
            2 * length * width * (own + wo.shape[0]), 2 * width * (own + wo.shape[0] + 4 * length)
        ),
        name="weight_grads",
    )(*normed, *d_qkv, *mixed, *g_all)


def per_device(
    arrivals,
    fresh_inputs,
    returning,
    loss_grads,
    stash_rows,
    forward_docs,
    backward_docs,
    norm_gain,
    w_query,
    w_key,
    w_value,
    w_out,
):
    section = lax.axis_index("section")
    last = lax.axis_size("section") - 1
    ticks = stash_rows.shape[1]
    wq, wk, wv, wo = w_query[0], w_key[0], w_value[0], w_out[0]
    gain = norm_gain

    stash = [mirrored(stash_rows[0, t]) for t in range(ticks)]
    x_own, g_own = arrivals[0], returning[0]
    g_wide = g_own.astype(F32)
    forward_list, backward_list, evict_list = [], [], []
    normed, d_qkv, mixed, g_all, gain_parts = [], [], [], [], []
    for t in range(ticks):
        x_entries = gather_x_first(x_own)
        g_entries = gather_x_first(g_own)
        z_entries = gather_x_first(stash[t])
        evict_list.append(mirrored(x_own))

        parts = forward_parts(t, x_entries, X_LAST, forward_docs, gain, wq, wk, wv, wo)
        attended = scatter_x_last(parts)
        produced = (x_own.astype(F32) + attended).astype(BF16)
        forward_list.append(produced)

        n, inverse, qkv, probs, m = recall(t, z_entries, backward_docs, gain, wq, wk, wv)
        back, d, g_whole, gain_part = backward_parts(
            g_entries, z_entries, X_LAST, inverse, qkv, probs, gain, wq, wk, wv, wo
        )
        normed.append(n)
        d_qkv.append(d)
        mixed.append(m)
        g_all.append(g_whole)
        gain_parts.append(gain_part)
        passed = g_wide + scatter_x_last(back)
        backward_list.append(passed)
        if t + 1 < ticks:
            x_own = jnp.where(section == 0, fresh_inputs[t], shifted(produced, 1))
            g_own = jnp.where(section == last, loss_grads[t], shifted(passed.astype(BF16), -1))
            g_wide = g_own.astype(F32)

    grads = weight_grads(normed, d_qkv, mixed, g_all, wq, wk, wv, wo)
    gain_sum = sum(gain_parts)
    near, far = gain_sum[:ROWS], gain_sum[ROWS:]
    near = near + x_flip(far)
    grad_gain = near[0] + sum(y_from(near[dy], -dy) for dy in range(1, ROWS))
    return (
        jnp.stack(forward_list)[None],
        jnp.stack(backward_list)[None],
        jnp.stack(evict_list)[None],
        *(g[None] for g in grads),
        grad_gain,
    )


def solution(mesh):
    return jax.shard_map(
        per_device,
        mesh=mesh,
        in_specs=(
            P("section", None, "tp"),
            P(None, None, "tp"),
            P("section", None, "tp"),
            P(None, None, "tp"),
            P("section", None, None, "tp"),
            P(),
            P(),
            P("section", None),
            P("section", None, "tp"),
            P("section", None, "tp"),
            P("section", None, "tp"),
            P("section", "tp", None),
        ),
        out_specs=(
            P("section", None, None, "tp"),
            P("section", None, None, "tp"),
            P("section", None, None, "tp"),
            P("section", None, "tp"),
            P("section", None, "tp"),
            P("section", None, "tp"),
            P("section", "tp", None),
            P("section", "tp"),
        ),
        check_vma=False,
    )
```

```python
import functools

import jax
import jax.numpy as jnp
from jax import lax
from jax.experimental import pallas as pl
from jax.experimental.pallas import tpu as pltpu
from jax.sharding import PartitionSpec as P

DH = 128
ROWS = 4
EPSILON = 1e-05
NEGATIVE = -1e30
F32 = jnp.float32
BF16 = jnp.bfloat16
EXTRA = 16
VMEM = pl.BlockSpec(memory_space=pltpu.VMEM)
ANY = pl.BlockSpec(memory_space=pl.ANY)
PARAMS = pltpu.CompilerParams(vmem_limit_bytes=48 * 1024 * 1024)


def shifted(block, distance):
    devices = range(lax.axis_size("section"))
    route = [(i - distance, i) for i in devices if i - distance in devices]
    return lax.ppermute(block, "section", route)


def mirrored(block):
    count = lax.axis_size("section")
    return lax.ppermute(block, "section", [(i, count - 1 - i) for i in range(count)])


def after(value, *earlier):
    return lax.optimization_barrier((value, *earlier))[0]


def x_flip(value):
    return lax.ppermute(value, "tp", [(i, i ^ ROWS) for i in range(2 * ROWS)])


def y_from(value, step):
    route = [(i, (i & ROWS) | ((i - step) % ROWS)) for i in range(2 * ROWS)]
    return lax.ppermute(value, "tp", route)


def gather(own, first=(), second=()):
    if first:
        own = after(own, *first)
    with jax.named_scope("other"):
        other = x_flip(own)
    with jax.named_scope("facing"):
        facing = y_from(own, 2)
    if second:
        other = after(other, *second)
    pair = jnp.stack([own, other])
    with jax.named_scope("up"):
        up = y_from(pair, 1)
    with jax.named_scope("down"):
        down = y_from(pair, 3)
    with jax.named_scope("cross"):
        cross = x_flip(facing)
    return [
        (own, None, 0, 0),
        (other, None, 1, 0),
        (facing, None, 0, 2),
        (up, 0, 0, 1),
        (up, 1, 1, 1),
        (down, 0, 0, 3),
        (down, 1, 1, 3),
        (cross, None, 1, 2),
    ]


SENDS = (((0, 1), (1, 1)), ((0, 3), (1, 3)), ((1, 2),), ((0, 0), (1, 0), (0, 2)))


def scatter(parts, second=()):
    up, down, far, kept = parts
    with jax.named_scope("up"):
        from_down = y_from(up, -1)
    with jax.named_scope("down"):
        from_up = y_from(down, -3)
    with jax.named_scope("cross"):
        crossed = x_flip(far[0])
    kept_b = after(kept, *second(crossed)) if second else kept
    beside = (kept_b[1].astype(F32) + from_down[1].astype(F32) + from_up[1].astype(F32)).astype(BF16)
    facing = (kept[2].astype(F32) + crossed.astype(F32)).astype(BF16)
    with jax.named_scope("other"):
        other = x_flip(beside)
    with jax.named_scope("facing"):
        opposite = y_from(facing, 2)
    mine = kept[0].astype(F32) + from_down[0].astype(F32) + from_up[0].astype(F32)
    return mine + other.astype(F32) + opposite.astype(F32), from_down


def place(dx, dy, share):
    me = lax.axis_index("tp")
    x = lax.div(me, ROWS)
    y = lax.rem(me, ROWS)
    far_x = 1 - x if dx else x
    index = far_x * ROWS + lax.rem(y + dy, ROWS)
    return pl.multiple_of(index * share, share)


def operands_of(entries):
    arrays, where = [], []
    for array, lead, dx, dy in entries:
        for i, known in enumerate(arrays):
            if known is array:
                break
        else:
            i = len(arrays)
            arrays.append(array)
        where.append((i, lead, dx, dy))
    return arrays, tuple(where)


def fetches(refs, where, whole, sems, first):
    share = whole.shape[1] // len(where)
    copies = []
    for i, (operand, lead, dx, dy) in enumerate(where):
        source = refs[operand].at[lead] if lead is not None else refs[operand]
        target = whole.at[:, pl.ds(place(dx, dy, share), share)]
        copies.append(pltpu.make_async_copy(source, target, sems.at[first + i]))
    for copy in copies:
        copy.start()
    return copies


def dot(a, b, dims=((1,), (0,))):
    return lax.dot_general(a, b, (dims, ((), ())), preferred_element_type=F32)


NT = ((1,), (1,))
TN = ((0,), (0,))


def mask_of(docs_ref, row):
    ids = docs_ref[pl.ds(row, 1), :]
    length = ids.shape[1]
    p = lax.broadcasted_iota(jnp.int32, (length, length), 0)
    r = lax.broadcasted_iota(jnp.int32, (length, length), 1)
    across = jnp.broadcast_to(ids, (length, length))
    down = jnp.sum(jnp.where(p == r, across, 0), axis=1, keepdims=True)
    return (across == down) & (r <= p)


def normalize_into(whole, gain_ref, normed_ref, parts):
    width = gain_ref.shape[1]
    share = width // parts
    total = None
    for j in range(parts):
        v = whole[:, j * share : (j + 1) * share].astype(F32)
        part = jnp.sum(v * v, axis=-1, keepdims=True)
        total = part if total is None else total + part
    inverse = lax.rsqrt(total / width + EPSILON)
    for j in range(parts):
        at = slice(j * share, (j + 1) * share)
        v = whole[:, at].astype(F32) * inverse
        normed_ref[:, at] = (v * gain_ref[:, at]).astype(BF16)
    return inverse


def attention(qkv, allowed, heads):
    k = qkv[:, heads * DH : (heads + 1) * DH]
    v = qkv[:, (heads + 1) * DH :]
    probs, mixed = [], []
    for h in range(heads):
        s = dot(qkv[:, h * DH : (h + 1) * DH], k, NT) * DH ** (-0.5)
        s = jnp.where(allowed, s, NEGATIVE)
        e = jnp.exp(s - jnp.max(s, axis=-1, keepdims=True))
        p = e / jnp.sum(e, axis=-1, keepdims=True)
        probs.append(p)
        mixed.append(dot(p.astype(BF16), v).astype(BF16))
    return probs, jnp.concatenate(mixed, axis=1)


def project(normed_ref, wq_ref, wk_ref, wv_ref):
    normed = normed_ref[...]
    q = dot(normed, wq_ref[...])
    kv = dot(normed, jnp.concatenate([wk_ref[...], wv_ref[...]], axis=1))
    return jnp.concatenate([q, kv], axis=1).astype(BF16)


def loads(sources, scratch, sems):
    copies = [
        pltpu.make_async_copy(source, target, sems.at[i])
        for i, (source, target) in enumerate(zip(sources, scratch))
    ]
    for copy in copies:
        copy.start()
    return copies


def forward_kernel(tick, where, layout, n_x, *refs):
    x_refs, refs = refs[:n_x], refs[n_x:]
    docs, gain, wq_hbm, wk_hbm, wv_hbm, wo_hbm = refs[:6]
    outs, refs = refs[6 : 6 + len(layout)], refs[6 + len(layout) :]
    whole, normed, wq, wk, wv, wo, sems = refs
    pieces = fetches(x_refs, where, whole, sems, 4)
    copies = loads((wq_hbm, wk_hbm, wv_hbm, wo_hbm), (wq, wk, wv, wo), sems)
    row = tick + lax.axis_size("section") - 1 - lax.axis_index("section")
    allowed = mask_of(docs, row)
    for copy in pieces:
        copy.wait()
    normalize_into(whole, gain, normed, len(where))
    for copy in copies[:3]:
        copy.wait()
    qkv = project(normed, wq, wk, wv)
    mixed = attention(qkv, allowed, wq.shape[1] // DH)[1]
    copies[3].wait()
    share = gain.shape[1] // len(where)
    for out, targets in zip(outs, layout):
        for lead, (dx, dy) in enumerate(targets):
            at = place(dx, dy, share)
            out[lead] = dot(mixed, wo[:, pl.ds(at, share)]).astype(BF16)


def recall_kernel(tick, where, n_x, *refs):
    x_refs, refs = refs[:n_x], refs[n_x:]
    docs, gain, wq_hbm, wk_hbm, wv_hbm = refs[:5]
    normed, inverse, qkv_out, probs_out, mixed_out = refs[5:10]
    whole, wq, wk, wv, sems = refs[10:]
    pieces = fetches(x_refs, where, whole, sems, 3)
    copies = loads((wq_hbm, wk_hbm, wv_hbm), (wq, wk, wv), sems)
    allowed = mask_of(docs, tick + lax.axis_index("section"))
    for copy in pieces:
        copy.wait()
    inverse[...] = normalize_into(whole, gain, normed, len(where))
    for copy in copies:
        copy.wait()
    qkv = project(normed, wq, wk, wv)
    probs, mixed = attention(qkv, allowed, wq.shape[1] // DH)
    qkv_out[...] = qkv
    mixed_out[...] = mixed
    for h, p in enumerate(probs):
        probs_out[h] = p


def backward_kernel(where_g, n_g, where_x, n_x, layout, extra, *refs):
    g_refs, refs = refs[:n_g], refs[n_g:]
    x_refs, refs = refs[:n_x], refs[n_x:]
    inverse_ref, qkv_ref, probs_ref, earlier, gain, wq_hbm, wk_hbm, wv_hbm, wo_hbm = refs[:9]
    outs, refs = refs[9 : 9 + len(layout)], refs[9 + len(layout) :]
    d_qkv_out, g_all, gain_out = refs[:3]
    whole, wq, wk, wv, wo, sems = refs[3:]
    pieces = fetches(g_refs, where_g, g_all, sems, 4)
    copies = loads((wo_hbm, wq_hbm, wk_hbm, wv_hbm), (wo, wq, wk, wv), sems)
    copies += fetches(x_refs, where_x, whole, sems, 4 + len(where_g))
    width = gain.shape[1]
    share = width // len(where_g)
    for copy in pieces:
        copy.wait()
    copies[0].wait()
    d_mixed = dot(g_all[...], wo[...], NT).astype(BF16)
    heads = wq.shape[1] // DH
    k = qkv_ref[:, heads * DH : (heads + 1) * DH]
    v = qkv_ref[:, (heads + 1) * DH :]
    d_parts = []
    d_k = d_v = None
    for h in range(heads):
        q = qkv_ref[:, h * DH : (h + 1) * DH]
        p = probs_ref[h]
        d_out = d_mixed[:, h * DH : (h + 1) * DH]
        d_p = dot(d_out, v, NT)
        inner = jnp.sum(d_p * p, axis=-1, keepdims=True)
        d_s = (p * (d_p - inner) * DH ** (-0.5)).astype(BF16)
        d_parts.append(dot(d_s, k).astype(BF16))
        more_k = dot(d_s, q, TN)
        more_v = dot(p.astype(BF16), d_out, TN)
        d_k = more_k if d_k is None else d_k + more_k
        d_v = more_v if d_v is None else d_v + more_v
    d_qkv = jnp.concatenate(d_parts + [d_k.astype(BF16), d_v.astype(BF16)], axis=1)
    d_qkv_out[...] = d_qkv
    row_total = jnp.sum(d_qkv.astype(F32) * qkv_ref[...].astype(F32), axis=-1, keepdims=True)
    row_mean = row_total / width
    inverse = inverse_ref[...]
    for copy in copies[1:]:
        copy.wait()
    length = inverse.shape[0]
    d_q, d_kv = d_qkv[:, : heads * DH], d_qkv[:, heads * DH :]
    for out, targets in zip(outs, layout):
        for lead, (dx, dy) in enumerate(targets):
            at = place(dx, dy, share)
            rows = pl.ds(at, share)
            w_kv = jnp.concatenate([wk[rows, :], wv[rows, :]], axis=1)
            d_normed = dot(d_q, wq[rows, :], NT) + dot(d_kv, w_kv, NT)
            unit = whole[:, rows].astype(F32) * inverse
            gain_sum = jnp.sum(d_normed * unit, axis=0, keepdims=True)
            target = dx * ROWS + dy
            d_unit = d_normed * gain[:, rows]
            out[lead, :length, :] = (inverse * (d_unit - unit * row_mean)).astype(BF16)
            if extra:
                gain_sum = gain_sum + earlier[target]
                high = gain_sum.astype(BF16)
                low = (gain_sum - high.astype(F32)).astype(BF16)
                row = lax.broadcasted_iota(jnp.int32, (extra, share), 0)
                terms = jnp.where(row == 0, high.astype(F32), jnp.where(row == 1, low.astype(F32), 0.0))
                out[lead, length:, :] = terms.astype(BF16)
            else:
                gain_out[target] = gain_sum
    if extra:
        gain_out[...] = earlier[...]


def grads_kernel(n0, n1, dq0, dq1, m0, m1, g0, g1, gq, gk, gv, go):
    d0, d1 = dq0[...], dq1[...]
    grad = dot(n0[...], d0, TN) + dot(n1[...], d1, TN)
    wide = gq.shape[1]
    gq[...] = grad[:, :wide].astype(BF16)
    gk[...] = grad[:, wide : wide + DH].astype(BF16)
    gv[...] = grad[:, wide + DH :].astype(BF16)
    go[...] = (dot(m0[...], g0[...], TN) + dot(m1[...], g1[...], TN)).astype(BF16)


def shape(dims, dtype=BF16):
    return jax.ShapeDtypeStruct(dims, dtype)


def cost(multiplies, moved):
    return pl.CostEstimate(flops=6 * multiplies, bytes_accessed=3 * moved, transcendentals=0)


def full_cost(multiplies, moved):
    return pl.CostEstimate(flops=2 * multiplies, bytes_accessed=moved, transcendentals=0)


def part_shapes(layout, length, share):
    return [shape((len(targets), length, share)) for targets in layout]


def scratch_for(more, *weights):
    return [pltpu.VMEM(w.shape, w.dtype) for w in weights] + [
        pltpu.SemaphoreType.DMA((len(weights) + more,))
    ]


def forward_parts(tick, entries, layout, docs, gain, wq, wk, wv, wo):
    arrays, where = operands_of(entries)
    length, share = entries[0][0].shape
    width = gain.shape[1]
    own = wq.shape[1] + wk.shape[1] + wv.shape[1]
    return pl.pallas_call(
        functools.partial(forward_kernel, tick, where, layout, len(arrays)),
        out_shape=part_shapes(layout, length, share),
        in_specs=[ANY] * len(arrays) + [VMEM] * 2 + [ANY] * 4,
        out_specs=[VMEM] * len(layout),
        scratch_shapes=[pltpu.VMEM((length, width), BF16)] * 2
        + scratch_for(len(where), wq, wk, wv, wo),
        compiler_params=PARAMS,
        cost_estimate=cost(length * width * (own + wo.shape[0]), 2 * width * (own + wo.shape[0])),
        name="forward",
    )(*arrays, docs, gain, wq, wk, wv, wo)


def recall(tick, entries, docs, gain, wq, wk, wv):
    arrays, where = operands_of(entries)
    length = entries[0][0].shape[0]
    width = gain.shape[1]
    own = wq.shape[1] + wk.shape[1] + wv.shape[1]
    return pl.pallas_call(
        functools.partial(recall_kernel, tick, where, len(arrays)),
        out_shape=[
            shape((length, width)),
            shape((length, 1), F32),
            shape((length, own)),
            shape((wq.shape[1] // DH, length, length), F32),
            shape((length, wq.shape[1])),
        ],
        in_specs=[ANY] * len(arrays) + [VMEM] * 2 + [ANY] * 3,
        out_specs=[VMEM] * 5,
        scratch_shapes=[pltpu.VMEM((length, width), BF16)] + scratch_for(len(where), wq, wk, wv),
        compiler_params=PARAMS,
        cost_estimate=cost(length * width * own, 2 * width * own),
        name="recall",
    )(*arrays, docs, gain, wq, wk, wv)


def backward_parts(
    entries_g, entries_x, layout, inverse, qkv, probs, earlier, gain, wq, wk, wv, wo, extra
):
    arrays_g, where_g = operands_of(entries_g)
    arrays_x, where_x = operands_of(entries_x)
    length, share = entries_g[0][0].shape
    width = gain.shape[1]
    own = qkv.shape[1]
    results = pl.pallas_call(
        functools.partial(
            backward_kernel, where_g, len(arrays_g), where_x, len(arrays_x), layout, extra
        ),
        out_shape=part_shapes(layout, length + extra, share)
        + [
            shape((length, own)),
            shape((length, width)),
            shape((width // share, 1, share), F32),
        ],
        in_specs=[ANY] * (len(arrays_g) + len(arrays_x)) + [VMEM] * 5 + [ANY] * 4,
        out_specs=[VMEM] * (len(layout) + 3),
        scratch_shapes=[pltpu.VMEM((length, width), BF16)]
        + scratch_for(len(where_g) + len(where_x), wq, wk, wv, wo),
        compiler_params=PARAMS,
        cost_estimate=cost(length * width * (own + wo.shape[0]), 2 * width * (own + wo.shape[0])),
        name="backward",
    )(*arrays_g, *arrays_x, inverse, qkv, probs, earlier, gain, wq, wk, wv, wo)
    parts = results[: len(layout)]
    return (parts, *results[len(layout) :])


def weight_grads(normed, d_qkv, mixed, g_all, wq, wk, wv, wo):
    length, width = normed[0].shape
    block = min(512, width)
    whole = lambda a: pl.BlockSpec(a.shape, lambda i: (0, 0))
    slab = pl.BlockSpec((length, block), lambda i: (0, i))
    rows = lambda w: pl.BlockSpec((block, w.shape[1]), lambda i: (i, 0))
    own = d_qkv[0].shape[1]
    return pl.pallas_call(
        grads_kernel,
        grid=(width // block,),
        out_shape=[shape(w.shape) for w in (wq, wk, wv, wo)],
        in_specs=[slab, slab, whole(d_qkv[0]), whole(d_qkv[0]), whole(mixed[0]), whole(mixed[0]), slab, slab],
        out_specs=[rows(wq), rows(wk), rows(wv), pl.BlockSpec((wo.shape[0], block), lambda i: (0, i))],
        compiler_params=PARAMS,
        cost_estimate=full_cost(
            2 * length * width * (own + wo.shape[0]), 2 * width * (own + wo.shape[0] + 4 * length)
        ),
        name="weight_grads",
    )(*normed, *d_qkv, *mixed, *g_all)


def per_device(
    arrivals,
    fresh_inputs,
    returning,
    loss_grads,
    stash_rows,
    forward_docs,
    backward_docs,
    norm_gain,
    w_query,
    w_key,
    w_value,
    w_out,
):
    section = lax.axis_index("section")
    last = lax.axis_size("section") - 1
    wq, wk, wv, wo = w_query[0], w_key[0], w_value[0], w_out[0]
    gain = norm_gain

    x0, g0 = arrivals[0], returning[0]
    length, share = x0.shape
    weights = (wq, wk, wv, wo)

    with jax.named_scope("gather_x0"):
        x_all = gather(x0)
    with jax.named_scope("gather_g0"):
        g_all = gather(g0)
    with jax.named_scope("stash"):
        z0, z1 = mirrored(stash_rows[0])
    with jax.named_scope("gather_z0"):
        z_all = gather(z0)

    parts = forward_parts(0, x_all, SENDS, forward_docs, gain, *weights)
    with jax.named_scope("scatter_y0"):
        attended, y_first = scatter(parts)
    n0, inverse, qkv, probs, m0 = recall(0, z_all, after(backward_docs, parts[0]), gain, wq, wk, wv)
    no_gain = jnp.zeros((2 * ROWS, 1, share), F32)
    back, dq0, full0, gain0 = backward_parts(
        g_all, z_all, SENDS, inverse, qkv, probs, no_gain, gain, *weights, 0
    )
    with jax.named_scope("scatter_d0"):
        returned, d_first = scatter(back)
    y0 = (x0.astype(F32) + attended).astype(BF16)
    d0 = g0.astype(F32) + returned
    with jax.named_scope("gather_z1"):
        z_all = gather(z1, first=(y_first,), second=(d_first,))

    with jax.named_scope("shift_x"):
        x1 = jnp.where(section == 0, fresh_inputs[0], shifted(y0, 1))
    with jax.named_scope("shift_g"):
        g1 = jnp.where(section == last, loss_grads[0], shifted(d0.astype(BF16), -1))
    with jax.named_scope("gather_g1"):
        g_all = gather(g1)
    with jax.named_scope("gather_x1"):
        x_all = gather(x1)

    n1, inverse, qkv, probs, m1 = recall(1, z_all, backward_docs, gain, wq, wk, wv)
    parts = forward_parts(1, x_all, SENDS, forward_docs, gain, *weights)
    back, dq1, full1, _ = backward_parts(
        g_all, z_all, SENDS, inverse, qkv, probs, gain0, gain, *weights, EXTRA
    )
    with jax.named_scope("scatter_y1"):
        attended, _ = scatter(parts)
    with jax.named_scope("evict"):
        evicted = mirrored(after(jnp.stack([x0, x1]), x_all[3][0]))
    y1 = (x1.astype(F32) + attended).astype(BF16)

    made = []

    def grads_beside(crossed):
        made.extend(
            weight_grads((after(n0, crossed), n1), (dq0, dq1), (m0, m1), (full0, full1), *weights)
        )
        return (made[1],)

    with jax.named_scope("scatter_d1"):
        returned, _ = scatter(back, grads_beside)
    d1 = g1.astype(F32) + returned[:length]
    grad_gain = returned[length : length + 1] + returned[length + 1 : length + 2]
    return (
        jnp.stack([y0, y1])[None],
        jnp.stack([d0, d1])[None],
        evicted[None],
        *(g[None] for g in made),
        grad_gain,
    )


def solution(mesh):
    return jax.shard_map(
        per_device,
        mesh=mesh,
        in_specs=(
            P("section", None, "tp"),
            P(None, None, "tp"),
            P("section", None, "tp"),
            P(None, None, "tp"),
            P("section", None, None, "tp"),
            P(),
            P(),
            P("section", None),
            P("section", None, "tp"),
            P("section", None, "tp"),
            P("section", None, "tp"),
            P("section", "tp", None),
        ),
        out_specs=(
            P("section", None, None, "tp"),
            P("section", None, None, "tp"),
            P("section", None, None, "tp"),
            P("section", None, "tp"),
            P("section", None, "tp"),
            P("section", None, "tp"),
            P("section", "tp", None),
            P("section", "tp"),
        ),
        check_vma=False,
    )
```

```python
import functools

import jax
import jax.numpy as jnp
from jax import lax
from jax.experimental import pallas as pl
from jax.experimental.pallas import tpu as pltpu
from jax.sharding import PartitionSpec as P

DH = 128
ROWS = 4
EPSILON = 1e-05
NEGATIVE = -1e30
F32 = jnp.float32
BF16 = jnp.bfloat16
EXTRA = 16
VMEM = pl.BlockSpec(memory_space=pltpu.VMEM)
ANY = pl.BlockSpec(memory_space=pl.ANY)
PARAMS = pltpu.CompilerParams(vmem_limit_bytes=48 * 1024 * 1024)


def shifted(block, distance):
    devices = range(lax.axis_size("section"))
    route = [(i - distance, i) for i in devices if i - distance in devices]
    return lax.ppermute(block, "section", route)


def mirrored(block):
    count = lax.axis_size("section")
    return lax.ppermute(block, "section", [(i, count - 1 - i) for i in range(count)])


def after(value, *earlier):
    return lax.optimization_barrier((value, *earlier))[0]


def x_flip(value):
    return lax.ppermute(value, "tp", [(i, i ^ ROWS) for i in range(2 * ROWS)])


def y_from(value, step):
    route = [(i, (i & ROWS) | ((i - step) % ROWS)) for i in range(2 * ROWS)]
    return lax.ppermute(value, "tp", route)


def gather(own, first=(), second=()):
    if first:
        own = after(own, *first)
    with jax.named_scope("other"):
        other = x_flip(own)
    with jax.named_scope("facing"):
        facing = y_from(own, 2)
    if second:
        other = after(other, *second)
    pair = jnp.stack([own, other])
    with jax.named_scope("up"):
        up = y_from(pair, 1)
    with jax.named_scope("down"):
        down = y_from(pair, 3)
    with jax.named_scope("cross"):
        cross = x_flip(facing)
    return [
        (own, None, 0, 0),
        (other, None, 1, 0),
        (facing, None, 0, 2),
        (up, 0, 0, 1),
        (up, 1, 1, 1),
        (down, 0, 0, 3),
        (down, 1, 1, 3),
        (cross, None, 1, 2),
    ]


SENDS = (((0, 1), (1, 1)), ((0, 3), (1, 3)), ((1, 2),), ((0, 0), (1, 0), (0, 2)))


def scatter(parts, second=()):
    up, down, far, kept = parts
    with jax.named_scope("up"):
        from_down = y_from(up, -1)
    with jax.named_scope("down"):
        from_up = y_from(down, -3)
    with jax.named_scope("cross"):
        crossed = x_flip(far[0])
    kept_b = after(kept, *second(crossed)) if second else kept
    beside = (kept_b[1].astype(F32) + from_down[1].astype(F32) + from_up[1].astype(F32)).astype(BF16)
    facing = (kept[2].astype(F32) + crossed.astype(F32)).astype(BF16)
    with jax.named_scope("other"):
        other = x_flip(beside)
    with jax.named_scope("facing"):
        opposite = y_from(facing, 2)
    mine = kept[0].astype(F32) + from_down[0].astype(F32) + from_up[0].astype(F32)
    return mine + other.astype(F32) + opposite.astype(F32), from_down


def place(dx, dy, share):
    me = lax.axis_index("tp")
    x = lax.div(me, ROWS)
    y = lax.rem(me, ROWS)
    far_x = 1 - x if dx else x
    index = far_x * ROWS + lax.rem(y + dy, ROWS)
    return pl.multiple_of(index * share, share)


def operands_of(entries):
    arrays, where = [], []
    for array, lead, dx, dy in entries:
        for i, known in enumerate(arrays):
            if known is array:
                break
        else:
            i = len(arrays)
            arrays.append(array)
        where.append((i, lead, dx, dy))
    return arrays, tuple(where)


def fetches(refs, where, whole, sems, first):
    share = whole.shape[1] // len(where)
    copies = []
    for i, (operand, lead, dx, dy) in enumerate(where):
        source = refs[operand].at[lead] if lead is not None else refs[operand]
        target = whole.at[:, pl.ds(place(dx, dy, share), share)]
        copies.append(pltpu.make_async_copy(source, target, sems.at[first + i]))
    for copy in copies:
        copy.start()
    return copies


def dot(a, b, dims=((1,), (0,))):
    return lax.dot_general(a, b, (dims, ((), ())), preferred_element_type=F32)


NT = ((1,), (1,))
TN = ((0,), (0,))


def mask_of(docs_ref, row):
    ids = docs_ref[pl.ds(row, 1), :]
    length = ids.shape[1]
    p = lax.broadcasted_iota(jnp.int32, (length, length), 0)
    r = lax.broadcasted_iota(jnp.int32, (length, length), 1)
    across = jnp.broadcast_to(ids, (length, length))
    down = jnp.sum(jnp.where(p == r, across, 0), axis=1, keepdims=True)
    return (across == down) & (r <= p)


def normalize_into(whole, gain_ref, normed_ref, parts):
    width = gain_ref.shape[1]
    share = width // parts
    total = None
    for j in range(parts):
        v = whole[:, j * share : (j + 1) * share].astype(F32)
        part = jnp.sum(v * v, axis=-1, keepdims=True)
        total = part if total is None else total + part
    inverse = lax.rsqrt(total / width + EPSILON)
    for j in range(parts):
        at = slice(j * share, (j + 1) * share)
        v = whole[:, at].astype(F32) * inverse
        normed_ref[:, at] = (v * gain_ref[:, at]).astype(BF16)
    return inverse


def stacked(rows, heads):
    return jnp.concatenate([rows[:, h * DH : (h + 1) * DH] for h in range(heads)], axis=0)


def beside(rows, heads):
    length = rows.shape[0] // heads
    return jnp.concatenate([rows[h * length : (h + 1) * length] for h in range(heads)], axis=1)


def attention(qkv, allowed, heads):
    k = qkv[:, heads * DH : (heads + 1) * DH]
    v = qkv[:, (heads + 1) * DH :]
    length = qkv.shape[0]
    s = dot(stacked(qkv, heads), k, NT) * DH ** (-0.5)
    s = jnp.where(allowed[None], s.reshape(heads, length, length), NEGATIVE)
    e = jnp.exp(s - jnp.max(s, axis=-1, keepdims=True))
    p = e * (1.0 / jnp.sum(e, axis=-1, keepdims=True))
    mixed = dot(p.astype(BF16).reshape(heads * length, length), v).astype(BF16)
    return p, beside(mixed, heads)


def project(normed_ref, wq_ref, wk_ref, wv_ref):
    normed = normed_ref[...]
    q = dot(normed, wq_ref[...])
    kv = dot(normed, jnp.concatenate([wk_ref[...], wv_ref[...]], axis=1))
    return jnp.concatenate([q, kv], axis=1).astype(BF16)


def loads(sources, scratch, sems):
    copies = [
        pltpu.make_async_copy(source, target, sems.at[i])
        for i, (source, target) in enumerate(zip(sources, scratch))
    ]
    for copy in copies:
        copy.start()
    return copies


def forward_kernel(tick, where, layout, n_x, *refs):
    x_refs, refs = refs[:n_x], refs[n_x:]
    docs, gain, wq_hbm, wk_hbm, wv_hbm, wo_hbm = refs[:6]
    outs, refs = refs[6 : 6 + len(layout)], refs[6 + len(layout) :]
    whole, normed, wq, wk, wv, wo, sems = refs
    pieces = fetches(x_refs, where, whole, sems, 4)
    copies = loads((wq_hbm, wk_hbm, wv_hbm, wo_hbm), (wq, wk, wv, wo), sems)
    row = tick + lax.axis_size("section") - 1 - lax.axis_index("section")
    allowed = mask_of(docs, row)
    for copy in pieces:
        copy.wait()
    normalize_into(whole, gain, normed, len(where))
    for copy in copies[:3]:
        copy.wait()
    qkv = project(normed, wq, wk, wv)
    mixed = attention(qkv, allowed, wq.shape[1] // DH)[1]
    copies[3].wait()
    share = gain.shape[1] // len(where)
    for out, targets in zip(outs, layout):
        for lead, (dx, dy) in enumerate(targets):
            at = place(dx, dy, share)
            out[lead] = dot(mixed, wo[:, pl.ds(at, share)]).astype(BF16)


def recall_kernel(tick, where, n_x, *refs):
    x_refs, refs = refs[:n_x], refs[n_x:]
    docs, gain, wq_hbm, wk_hbm, wv_hbm = refs[:5]
    normed, inverse, qkv_out, probs_out, mixed_out = refs[5:10]
    whole, wq, wk, wv, sems = refs[10:]
    pieces = fetches(x_refs, where, whole, sems, 3)
    copies = loads((wq_hbm, wk_hbm, wv_hbm), (wq, wk, wv), sems)
    allowed = mask_of(docs, tick + lax.axis_index("section"))
    for copy in pieces:
        copy.wait()
    inverse[...] = normalize_into(whole, gain, normed, len(where))
    for copy in copies:
        copy.wait()
    qkv = project(normed, wq, wk, wv)
    probs, mixed = attention(qkv, allowed, wq.shape[1] // DH)
    qkv_out[...] = qkv
    mixed_out[...] = mixed
    probs_out[...] = probs


def backward_kernel(where_g, n_g, where_x, n_x, layout, extra, *refs):
    g_refs, refs = refs[:n_g], refs[n_g:]
    x_refs, refs = refs[:n_x], refs[n_x:]
    inverse_ref, qkv_ref, probs_ref, earlier, gain, wq_hbm, wk_hbm, wv_hbm, wo_hbm = refs[:9]
    outs, refs = refs[9 : 9 + len(layout)], refs[9 + len(layout) :]
    d_qkv_out, g_all, gain_out = refs[:3]
    whole, wq, wk, wv, wo, sems = refs[3:]
    pieces = fetches(g_refs, where_g, g_all, sems, 4)
    copies = loads((wo_hbm, wq_hbm, wk_hbm, wv_hbm), (wo, wq, wk, wv), sems)
    copies += fetches(x_refs, where_x, whole, sems, 4 + len(where_g))
    width = gain.shape[1]
    share = width // len(where_g)
    for copy in pieces:
        copy.wait()
    copies[0].wait()
    d_mixed = dot(g_all[...], wo[...], NT).astype(BF16)
    heads = wq.shape[1] // DH
    k = qkv_ref[:, heads * DH : (heads + 1) * DH]
    v = qkv_ref[:, (heads + 1) * DH :]
    length = d_mixed.shape[0]
    d_out = stacked(d_mixed, heads)
    p = probs_ref[...].reshape(heads * length, length)
    d_p = dot(d_out, v, NT)
    inner = jnp.sum(d_p * p, axis=-1, keepdims=True)
    d_s = (p * (d_p - inner) * DH ** (-0.5)).astype(BF16)
    d_q = beside(dot(d_s, k).astype(BF16), heads)
    d_k = dot(d_s, stacked(qkv_ref[:, : heads * DH], heads), TN).astype(BF16)
    d_v = dot(p.astype(BF16), d_out, TN).astype(BF16)
    d_qkv = jnp.concatenate([d_q, d_k, d_v], axis=1)
    d_qkv_out[...] = d_qkv
    row_total = jnp.sum(d_qkv.astype(F32) * qkv_ref[...].astype(F32), axis=-1, keepdims=True)
    row_mean = row_total / width
    inverse = inverse_ref[...]
    for copy in copies[1:]:
        copy.wait()
    length = inverse.shape[0]
    d_q, d_kv = d_qkv[:, : heads * DH], d_qkv[:, heads * DH :]
    for out, targets in zip(outs, layout):
        for lead, (dx, dy) in enumerate(targets):
            at = place(dx, dy, share)
            rows = pl.ds(at, share)
            w_kv = jnp.concatenate([wk[rows, :], wv[rows, :]], axis=1)
            d_normed = dot(d_q, wq[rows, :], NT) + dot(d_kv, w_kv, NT)
            unit = whole[:, rows].astype(F32) * inverse
            gain_sum = jnp.sum(d_normed * unit, axis=0, keepdims=True)
            target = dx * ROWS + dy
            d_unit = d_normed * gain[:, rows]
            out[lead, :length, :] = (inverse * (d_unit - unit * row_mean)).astype(BF16)
            if extra:
                gain_sum = gain_sum + earlier[target]
                high = gain_sum.astype(BF16)
                low = (gain_sum - high.astype(F32)).astype(BF16)
                row = lax.broadcasted_iota(jnp.int32, (extra, share), 0)
                terms = jnp.where(row == 0, high.astype(F32), jnp.where(row == 1, low.astype(F32), 0.0))
                out[lead, length:, :] = terms.astype(BF16)
            else:
                gain_out[target] = gain_sum
    if extra:
        gain_out[...] = earlier[...]


def grads_kernel(n0, n1, dq0, dq1, m0, m1, g0, g1, gq, gk, gv, go):
    d0, d1 = dq0[...], dq1[...]
    grad = dot(n0[...], d0, TN) + dot(n1[...], d1, TN)
    wide = gq.shape[1]
    gq[...] = grad[:, :wide].astype(BF16)
    gk[...] = grad[:, wide : wide + DH].astype(BF16)
    gv[...] = grad[:, wide + DH :].astype(BF16)
    go[...] = (dot(m0[...], g0[...], TN) + dot(m1[...], g1[...], TN)).astype(BF16)


def shape(dims, dtype=BF16):
    return jax.ShapeDtypeStruct(dims, dtype)


def cost(multiplies, moved):
    return pl.CostEstimate(flops=6 * multiplies, bytes_accessed=3 * moved, transcendentals=0)


def full_cost(multiplies, moved):
    return pl.CostEstimate(flops=2 * multiplies, bytes_accessed=moved, transcendentals=0)


def part_shapes(layout, length, share):
    return [shape((len(targets), length, share)) for targets in layout]


def scratch_for(more, *weights):
    return [pltpu.VMEM(w.shape, w.dtype) for w in weights] + [
        pltpu.SemaphoreType.DMA((len(weights) + more,))
    ]


def forward_parts(tick, entries, layout, docs, gain, wq, wk, wv, wo):
    arrays, where = operands_of(entries)
    length, share = entries[0][0].shape
    width = gain.shape[1]
    own = wq.shape[1] + wk.shape[1] + wv.shape[1]
    return pl.pallas_call(
        functools.partial(forward_kernel, tick, where, layout, len(arrays)),
        out_shape=part_shapes(layout, length, share),
        in_specs=[ANY] * len(arrays) + [VMEM] * 2 + [ANY] * 4,
        out_specs=[VMEM] * len(layout),
        scratch_shapes=[pltpu.VMEM((length, width), BF16)] * 2
        + scratch_for(len(where), wq, wk, wv, wo),
        compiler_params=PARAMS,
        cost_estimate=cost(length * width * (own + wo.shape[0]), 2 * width * (own + wo.shape[0])),
        name="forward",
    )(*arrays, docs, gain, wq, wk, wv, wo)


def recall(tick, entries, docs, gain, wq, wk, wv):
    arrays, where = operands_of(entries)
    length = entries[0][0].shape[0]
    width = gain.shape[1]
    own = wq.shape[1] + wk.shape[1] + wv.shape[1]
    return pl.pallas_call(
        functools.partial(recall_kernel, tick, where, len(arrays)),
        out_shape=[
            shape((length, width)),
            shape((length, 1), F32),
            shape((length, own)),
            shape((wq.shape[1] // DH, length, length), F32),
            shape((length, wq.shape[1])),
        ],
        in_specs=[ANY] * len(arrays) + [VMEM] * 2 + [ANY] * 3,
        out_specs=[VMEM] * 5,
        scratch_shapes=[pltpu.VMEM((length, width), BF16)] + scratch_for(len(where), wq, wk, wv),
        compiler_params=PARAMS,
        cost_estimate=cost(length * width * own, 2 * width * own),
        name="recall",
    )(*arrays, docs, gain, wq, wk, wv)


def backward_parts(
    entries_g, entries_x, layout, inverse, qkv, probs, earlier, gain, wq, wk, wv, wo, extra
):
    arrays_g, where_g = operands_of(entries_g)
    arrays_x, where_x = operands_of(entries_x)
    length, share = entries_g[0][0].shape
    width = gain.shape[1]
    own = qkv.shape[1]
    results = pl.pallas_call(
        functools.partial(
            backward_kernel, where_g, len(arrays_g), where_x, len(arrays_x), layout, extra
        ),
        out_shape=part_shapes(layout, length + extra, share)
        + [
            shape((length, own)),
            shape((length, width)),
            shape((width // share, 1, share), F32),
        ],
        in_specs=[ANY] * (len(arrays_g) + len(arrays_x)) + [VMEM] * 5 + [ANY] * 4,
        out_specs=[VMEM] * (len(layout) + 3),
        scratch_shapes=[pltpu.VMEM((length, width), BF16)]
        + scratch_for(len(where_g) + len(where_x), wq, wk, wv, wo),
        compiler_params=PARAMS,
        cost_estimate=cost(length * width * (own + wo.shape[0]), 2 * width * (own + wo.shape[0])),
        name="backward",
    )(*arrays_g, *arrays_x, inverse, qkv, probs, earlier, gain, wq, wk, wv, wo)
    parts = results[: len(layout)]
    return (parts, *results[len(layout) :])


def weight_grads(normed, d_qkv, mixed, g_all, wq, wk, wv, wo):
    length, width = normed[0].shape
    block = min(512, width)
    whole = lambda a: pl.BlockSpec(a.shape, lambda i: (0, 0))
    slab = pl.BlockSpec((length, block), lambda i: (0, i))
    rows = lambda w: pl.BlockSpec((block, w.shape[1]), lambda i: (i, 0))
    own = d_qkv[0].shape[1]
    return pl.pallas_call(
        grads_kernel,
        grid=(width // block,),
        out_shape=[shape(w.shape) for w in (wq, wk, wv, wo)],
        in_specs=[slab, slab, whole(d_qkv[0]), whole(d_qkv[0]), whole(mixed[0]), whole(mixed[0]), slab, slab],
        out_specs=[rows(wq), rows(wk), rows(wv), pl.BlockSpec((wo.shape[0], block), lambda i: (0, i))],
        compiler_params=PARAMS,
        cost_estimate=full_cost(
            2 * length * width * (own + wo.shape[0]), 2 * width * (own + wo.shape[0] + 4 * length)
        ),
        name="weight_grads",
    )(*normed, *d_qkv, *mixed, *g_all)


def per_device(
    arrivals,
    fresh_inputs,
    returning,
    loss_grads,
    stash_rows,
    forward_docs,
    backward_docs,
    norm_gain,
    w_query,
    w_key,
    w_value,
    w_out,
):
    section = lax.axis_index("section")
    last = lax.axis_size("section") - 1
    wq, wk, wv, wo = w_query[0], w_key[0], w_value[0], w_out[0]
    gain = norm_gain

    x0, g0 = arrivals[0], returning[0]
    length, share = x0.shape
    weights = (wq, wk, wv, wo)

    with jax.named_scope("gather_x0"):
        x_all = gather(x0)
    with jax.named_scope("gather_g0"):
        g_all = gather(g0)
    with jax.named_scope("stash"):
        z0, z1 = mirrored(stash_rows[0])
    with jax.named_scope("gather_z0"):
        z_all = gather(z0)

    parts = forward_parts(0, x_all, SENDS, forward_docs, gain, *weights)
    with jax.named_scope("scatter_y0"):
        attended, y_first = scatter(parts)
    n0, inverse, qkv, probs, m0 = recall(0, z_all, after(backward_docs, parts[0]), gain, wq, wk, wv)
    no_gain = jnp.zeros((2 * ROWS, 1, share), F32)
    back, dq0, full0, gain0 = backward_parts(
        g_all, z_all, SENDS, inverse, qkv, probs, no_gain, gain, *weights, 0
    )
    with jax.named_scope("scatter_d0"):
        returned, _ = scatter(back)
    y0 = (x0.astype(F32) + attended).astype(BF16)
    d0 = g0.astype(F32) + returned
    with jax.named_scope("gather_z1"):
        z_all = gather(z1, first=(z_all[3][0],), second=(y_first,))

    with jax.named_scope("shift_x"):
        x1 = jnp.where(section == 0, fresh_inputs[0], shifted(y0, 1))
    with jax.named_scope("shift_g"):
        g1 = jnp.where(section == last, loss_grads[0], shifted(d0.astype(BF16), -1))
    with jax.named_scope("gather_g1"):
        g_all = gather(g1)
    with jax.named_scope("gather_x1"):
        x_all = gather(x1)

    n1, inverse, qkv, probs, m1 = recall(1, z_all, backward_docs, gain, wq, wk, wv)
    parts = forward_parts(1, x_all, SENDS, forward_docs, gain, *weights)
    back, dq1, full1, _ = backward_parts(
        g_all, z_all, SENDS, inverse, qkv, probs, gain0, gain, *weights, EXTRA
    )
    with jax.named_scope("scatter_y1"):
        attended, _ = scatter(parts)
    with jax.named_scope("evict"):
        evicted = mirrored(after(jnp.stack([x0, x1]), back[0]))
    y1 = (x1.astype(F32) + attended).astype(BF16)

    made = []

    def grads_beside(crossed):
        made.extend(
            weight_grads((after(n0, crossed), n1), (dq0, dq1), (m0, m1), (full0, full1), *weights)
        )
        return (made[1],)

    with jax.named_scope("scatter_d1"):
        returned, _ = scatter(back, grads_beside)
    d1 = g1.astype(F32) + returned[:length]
    grad_gain = returned[length : length + 1] + returned[length + 1 : length + 2]
    return (
        jnp.stack([y0, y1])[None],
        jnp.stack([d0, d1])[None],
        evicted[None],
        *(g[None] for g in made),
        grad_gain,
    )


def solution(mesh):
    return jax.shard_map(
        per_device,
        mesh=mesh,
        in_specs=(
            P("section", None, "tp"),
            P(None, None, "tp"),
            P("section", None, "tp"),
            P(None, None, "tp"),
            P("section", None, None, "tp"),
            P(),
            P(),
            P("section", None),
            P("section", None, "tp"),
            P("section", None, "tp"),
            P("section", None, "tp"),
            P("section", "tp", None),
        ),
        out_specs=(
            P("section", None, None, "tp"),
            P("section", None, None, "tp"),
            P("section", None, None, "tp"),
            P("section", None, "tp"),
            P("section", None, "tp"),
            P("section", None, "tp"),
            P("section", "tp", None),
            P("section", "tp"),
        ),
        check_vma=False,
    )
```
